512 devices in a mesh: batch: 8 (over x, core), seq: 64 (over z, y).
Axes of the slice: x: 4, y: 4, z: 16, core: 2. Of those that a mesh axis runs over, the one named last changes fastest.
Arguments:
- query_nope: bfloat16 [8, 2, 16384], P('batch', None, 'seq'), may hold values from -6 to 6
- query_rope: bfloat16 [8, 2, 8192], P('batch', None, 'seq'), may hold values from -10 to 10
- latent_cache: bfloat16 [8, 65536, 576], P('batch', 'seq'), may hold values from -10 to 10
- lengths: int32 [8], P('batch'), may hold values from 16384 to 65536
- key_up: bfloat16 [128, 128, 512], P('seq', 'batch'), may hold values from -0.5 to 0.5
- value_up: bfloat16 [128, 512, 128], P('seq', 'batch'), may hold values from -1.5 to 1.5
Outputs:
- attended: bfloat16 [8, 2, 16384], P('batch', None, 'seq')
The draws below stay inside these ranges and needn't reach their ends.
All inputs are finite; a program needn't handle non-finite values.
Results may differ from the reference program's by a relative error of at most 0.04.
Values may be sent and summed in bfloat16 or wider, within the bound.
No kernel may reach another device: no remote copies, remote signals or barrier semaphores. Data moves between devices by JAX's collectives and lax.ppermute only.
A program may use at most 128 MiB of HBM per device.

```python
import math
import jax
import jax.numpy as jnp
from jax import lax

H = 128
NOPE = 128
ROPE = 64
LATENT = 512
QLEN = 2
BATCH = 8
CONTEXT = 65536


def draw_latent_cache(key, part):
    key = jax.random.fold_in(key, 11)
    shape = (BATCH, CONTEXT, LATENT + ROPE)
    base = jax.random.truncated_normal(key, -6.0, 6.0, shape, jnp.float32)
    return base.astype(jnp.bfloat16)


def draw_query_rope(key, part):
    key = jax.random.fold_in(key, 13)
    base_key = jax.random.fold_in(key, 0)
    shape = (BATCH, QLEN, H, ROPE)
    base = jax.random.truncated_normal(base_key, -6.0, 6.0, shape, jnp.float32)
    return base.reshape(BATCH, QLEN, H * ROPE).astype(jnp.bfloat16)


def draw_lengths(key, part):
    key = jax.random.fold_in(key, 7)
    first_key, pick_key = jax.random.split(key)
    values = jax.random.randint(first_key, (BATCH,), CONTEXT // 4, CONTEXT + 1)
    chosen_row = jax.random.randint(pick_key, (), 0, BATCH)
    return values.at[chosen_row].set(CONTEXT).astype(jnp.int32)


def block_scale(rng, shape, cuts, low, top_value):
    def one(dim, shards_of):
        draws = jax.random.uniform(jax.random.fold_in(jax.random.fold_in(rng, 6), dim), (shards_of,), jnp.float32, low / len(cuts), top_value / len(cuts))
        return jnp.repeat(jnp.exp(draws), shape[dim] // shards_of).reshape((-1,) + (1,) * (len(shape) - dim - 1))

    gain = one(*cuts[0])
    for cut in cuts[1:]:
        gain = gain * one(*cut)
    return gain


def centred(rng, extent, scale, most, cuts=(), held_as=jnp.bfloat16):
    level = block_scale(rng, extent, cuts, -0.22, 0.18) if cuts else 1.0
    entries = jax.random.normal(rng, extent, jnp.float32) * scale * level
    return jnp.minimum(jnp.maximum(entries, -most), most).astype(held_as)


def setup_inputs(seed: int = 0) -> dict:
    seeds = jax.random.split(jax.random.key(seed), 7)
    return {
        "query_nope": centred(seeds[0], (BATCH, QLEN, H * NOPE), 1.0, 6.0, ((0, 8), (2, 64))),
        "query_rope": draw_query_rope(jax.random.fold_in(seeds[6], 71), 0),
        "latent_cache": draw_latent_cache(jax.random.fold_in(seeds[6], 71), 0),
        "lengths": draw_lengths(jax.random.fold_in(seeds[6], 71), 0),
        "key_up": centred(seeds[4], (H, NOPE, LATENT), NOPE ** -0.5, 0.5, ((0, 64), (1, 8))),
        "value_up": centred(seeds[5], (H, LATENT, NOPE), (LATENT // 32) ** -0.5, 1.5, ((0, 64), (1, 8))),
    }


def reference(query_nope, query_rope, latent_cache, lengths, key_up, value_up):
    nope_query = query_nope.reshape(BATCH, QLEN, H, NOPE).astype(jnp.float32)
    absorbed = jnp.einsum('bthn,hnl->bthl', nope_query, key_up.astype(jnp.float32)).astype(jnp.bfloat16)
    rotary = query_rope.reshape(BATCH, QLEN, H, ROPE)
    query = jnp.concatenate([absorbed, rotary], axis=-1)
    scale = 1.0 / math.sqrt(NOPE + ROPE)

    def attend_row(packed):
        row_query, row_cache, length = packed
        scores = jnp.einsum('thd,cd->thc', row_query.astype(jnp.float32), row_cache.astype(jnp.float32)) * scale
        positions = jnp.arange(CONTEXT).astype(jnp.int32)
        limits = length - QLEN + 1 + jnp.arange(QLEN).astype(jnp.int32)
        visible = positions[None, None, :] < limits[:, None, None]
        scores = jnp.where(visible, scores, -1e+30)
        row_max = lax.optimization_barrier(jnp.max(scores, axis=-1, keepdims=True))
        weights = jnp.where(visible, jnp.exp(scores - row_max), 0.0)
        totals = lax.optimization_barrier(jnp.sum(weights, axis=-1))
        rounded = weights.astype(jnp.bfloat16)
        summed = jnp.einsum('thc,cl->thl', rounded.astype(jnp.float32), row_cache[:, :LATENT].astype(jnp.float32))
        return (summed / totals[..., None]).astype(jnp.bfloat16)
    latent_out = lax.map(attend_row, (query, latent_cache, lengths))
    attended = jnp.einsum('bthl,hlv->bthv', latent_out.astype(jnp.float32), value_up.astype(jnp.float32))
    return attended.astype(jnp.bfloat16).reshape(BATCH, QLEN, H * NOPE)
```

```python
import functools
import math

import jax
import jax.numpy as jnp
from jax import lax
from jax.experimental import pallas as pl
from jax.experimental.pallas import tpu as pltpu
from jax.sharding import PartitionSpec as P

VMEM = pl.BlockSpec(memory_space=pltpu.VMEM)
SMEM = pl.BlockSpec(memory_space=pltpu.SMEM)
PARAMS = pltpu.CompilerParams(vmem_limit_bytes=24 * 1024 * 1024)
F32 = jnp.float32
BF16 = jnp.bfloat16
HIDDEN = -1e30


def split3(x):
    high = x.astype(BF16).astype(F32)
    rest = x - high
    mid = rest.astype(BF16).astype(F32)
    return high, mid, (rest - mid).astype(BF16).astype(F32)


def pack_kernel(key_ref, value_ref, out_ref):
    heads, depth, latent = key_ref.shape
    key = jnp.concatenate(
        [key_ref[:, :, c : c + 128].reshape(heads * depth, 128) for c in range(0, latent, 128)], 0
    )
    value = value_ref[...].reshape(-1, 128)
    both = jnp.concatenate([key, value], 0)
    for i in range(out_ref.shape[0]):
        out_ref[i] = both


def absorb_kernel(heads, latent, parts_ref, nope_ref, rope_ref, out_ref):
    tokens = nope_ref.shape[1]
    head_width = nope_ref.shape[2] // heads
    rope_width = rope_ref.shape[2] // heads
    groups = parts_ref.shape[0]
    depth = head_width // groups
    blocks = []
    for c in range(latent // 128):
        rows = [
            parts_ref[:, (c * heads + h) * depth : (c * heads + h + 1) * depth, :].reshape(
                head_width, 128
            )
            for h in range(heads)
        ]
        blocks.append(jnp.concatenate(rows, 0))
    keys = jnp.concatenate(blocks, 1)
    row = lax.broadcasted_iota(jnp.int32, (8, heads * head_width), 0)
    col = lax.broadcasted_iota(jnp.int32, (8, heads * head_width), 1)
    nope = nope_ref[0].astype(F32)
    spread = jnp.zeros(row.shape, F32)
    for t in range(tokens):
        spread = jnp.where(row // heads == t, nope[t : t + 1], spread)
    spread = jnp.where(row % heads == col // head_width, spread, 0.0)
    absorbed = jnp.dot(spread.astype(BF16), keys, preferred_element_type=F32)
    rope = rope_ref[0].astype(F32)
    row = lax.broadcasted_iota(jnp.int32, (8, 128), 0)
    col = lax.broadcasted_iota(jnp.int32, (8, 128), 1)
    turned = jnp.zeros(row.shape, F32)
    for t in range(tokens):
        for h in range(heads):
            moved = rope[t : t + 1]
            if h:
                moved = pltpu.roll(moved, 128 - h * rope_width, 1)
            turned = jnp.where(row == t * heads + h, moved, turned)
    turned = jnp.where(col < rope_width, turned, 0.0)
    local = jnp.concatenate([absorbed, turned], 1)[: tokens * heads]
    out_ref[...] = jnp.broadcast_to(local[None], out_ref.shape).astype(BF16)


def attend_kernel(heads, tokens, scale, latent, query_ref, cache_ref, length_ref, out_ref):
    rows = query_ref.shape[0]
    block_len, width = cache_ref.shape
    contract = (((1,), (1,)), ((), ()))
    scores = lax.dot_general(
        query_ref[:, :latent], cache_ref[:, :latent], contract, preferred_element_type=F32
    )
    scores += lax.dot_general(
        query_ref[:, latent:width], cache_ref[:, latent:width], contract, preferred_element_type=F32
    )
    scores = scores * scale
    limit = length_ref[0] - tokens + 1 - lax.axis_index("seq") * block_len
    row = lax.broadcasted_iota(jnp.int32, (rows, 1), 0)
    limits = limit + (row // heads) % tokens
    visible = lax.broadcasted_iota(jnp.int32, (rows, block_len), 1) < limits
    scores = jnp.where(visible, scores, HIDDEN)
    peak = jnp.max(scores, axis=1, keepdims=True)
    weights = jnp.where(visible, jnp.exp(scores - peak), 0.0)
    total = jnp.sum(weights, axis=1, keepdims=True)
    summed = jnp.dot(weights.astype(BF16), cache_ref[:, :latent], preferred_element_type=F32)
    out_ref[:, :latent] = summed.astype(BF16)
    lane = lax.broadcasted_iota(jnp.int32, (rows, 128), 1)
    stats = jnp.zeros((rows, 128), F32)
    for i, term in enumerate(split3(peak) + split3(total)):
        stats = jnp.where(lane == i, term, stats)
    out_ref[:, latent:] = stats.astype(BF16)


def combine_kernel(heads, tokens, latent, sums_ref, parts_ref, out_ref):
    stats = sums_ref[:, :, latent:].astype(F32)
    peak = stats[:, :, 0:1] + stats[:, :, 1:2] + stats[:, :, 2:3]
    total = stats[:, :, 3:4] + stats[:, :, 4:5] + stats[:, :, 5:6]
    top = jnp.max(peak, axis=0, keepdims=True)
    factor = jnp.exp(peak - top)
    total = jnp.sum(factor * total, axis=0)
    summed = jnp.sum(factor * sums_ref[:, :, :latent].astype(F32), axis=0)
    mixed = (summed / total).astype(BF16)
    groups, rows = parts_ref.shape[0], parts_ref.shape[1]
    depth = latent // groups
    first = rows - heads * depth
    values = jnp.concatenate(
        [
            parts_ref[:, first + h * depth : first + (h + 1) * depth, :].reshape(latent, 128)
            for h in range(heads)
        ],
        1,
    )
    out = jnp.dot(mixed, values, preferred_element_type=F32)
    for t in range(tokens):
        for h in range(heads):
            out_ref[0, t : t + 1, h * 128 : (h + 1) * 128] = out[
                t * heads + h : t * heads + h + 1, h * 128 : (h + 1) * 128
            ].astype(BF16)


def call(kernel, shape, count, specs=None):
    return pl.pallas_call(
        kernel,
        out_shape=jax.ShapeDtypeStruct(shape, BF16),
        in_specs=specs or [VMEM] * count,
        out_specs=VMEM,
        compiler_params=PARAMS,
    )


def body(groups, owners, query_nope, query_rope, latent_cache, lengths, key_up, value_up):
    heads, depth, latent = key_up.shape
    tokens = query_nope.shape[1]
    head_width = query_nope.shape[2] // heads
    rope_width = query_rope.shape[2] // heads
    per_owner = tokens * heads
    wide = latent + 128
    part_rows = (key_up.size + value_up.size) // 128
    copies = call(pack_kernel, (groups, part_rows, 128), 2)(key_up, value_up)
    parts = lax.all_to_all(copies, "batch", 0, 0, tiled=True)
    queries = call(
        functools.partial(absorb_kernel, heads, latent), (owners, per_owner, wide), 3
    )(parts, query_nope, query_rope)
    queries = lax.all_to_all(queries, "seq", 0, 0, tiled=True)
    scale = 1.0 / math.sqrt(head_width + rope_width)
    sums = call(
        functools.partial(attend_kernel, heads, tokens, scale, latent),
        (owners * per_owner, wide),
        3,
        [VMEM, VMEM, SMEM],
    )(queries.reshape(owners * per_owner, wide), latent_cache[0], lengths)
    sums = lax.all_to_all(sums.reshape(owners, per_owner, wide), "seq", 0, 0, tiled=True)
    return call(
        functools.partial(combine_kernel, heads, tokens, latent),
        (1, tokens, heads * 128),
        2,
    )(sums, parts)


def solution(mesh):
    in_specs = (
        P("batch", None, "seq"),
        P("batch", None, "seq"),
        P("batch", "seq", None),
        P("batch"),
        P("seq", "batch", None),
        P("seq", "batch", None),
    )
    out_specs = P("batch", None, "seq")
    run = functools.partial(body, mesh.shape["batch"], mesh.shape["seq"])
    return jax.shard_map(run, mesh=mesh, in_specs=in_specs, out_specs=out_specs, check_vma=False)
```

```python
import functools
import math

import jax
import jax.numpy as jnp
from jax import lax
from jax.experimental import pallas as pl
from jax.experimental.pallas import tpu as pltpu
from jax.sharding import Mesh
from jax.sharding import PartitionSpec as P

VMEM = pl.BlockSpec(memory_space=pltpu.VMEM)
SMEM = pl.BlockSpec(memory_space=pltpu.SMEM)
PARAMS = pltpu.CompilerParams(vmem_limit_bytes=24 * 1024 * 1024)
F32 = jnp.float32
BF16 = jnp.bfloat16
HIDDEN = -1e30


def split3(x):
    high = x.astype(BF16).astype(F32)
    rest = x - high
    mid = rest.astype(BF16).astype(F32)
    return high, mid, (rest - mid).astype(BF16).astype(F32)


def pack_kernel(key_ref, value_ref, out_ref):
    heads, depth, latent = key_ref.shape
    key = jnp.concatenate(
        [key_ref[:, :, c : c + 128].reshape(heads * depth, 128) for c in range(0, latent, 128)], 0
    )
    value = value_ref[...].reshape(-1, 128)
    both = jnp.concatenate([key, value], 0)
    for i in range(out_ref.shape[0]):
        out_ref[i] = both


def absorb_kernel(heads, latent, parts_ref, nope_ref, rope_ref, out_ref):
    tokens = nope_ref.shape[1]
    head_width = nope_ref.shape[2] // heads
    rope_width = rope_ref.shape[2] // heads
    groups = parts_ref.shape[0]
    depth = head_width // groups
    blocks = []
    for c in range(latent // 128):
        rows = [
            parts_ref[:, (c * heads + h) * depth : (c * heads + h + 1) * depth, :].reshape(
                head_width, 128
            )
            for h in range(heads)
        ]
        blocks.append(jnp.concatenate(rows, 0))
    keys = jnp.concatenate(blocks, 1)
    row = lax.broadcasted_iota(jnp.int32, (8, heads * head_width), 0)
    col = lax.broadcasted_iota(jnp.int32, (8, heads * head_width), 1)
    nope = nope_ref[0].astype(F32)
    spread = jnp.zeros(row.shape, F32)
    for t in range(tokens):
        spread = jnp.where(row // heads == t, nope[t : t + 1], spread)
    spread = jnp.where(row % heads == col // head_width, spread, 0.0)
    absorbed = jnp.dot(spread.astype(BF16), keys, preferred_element_type=F32)
    rope = rope_ref[0].astype(F32)
    row = lax.broadcasted_iota(jnp.int32, (8, 128), 0)
    col = lax.broadcasted_iota(jnp.int32, (8, 128), 1)
    turned = jnp.zeros(row.shape, F32)
    for t in range(tokens):
        for h in range(heads):
            moved = rope[t : t + 1]
            if h:
                moved = pltpu.roll(moved, 128 - h * rope_width, 1)
            turned = jnp.where(row == t * heads + h, moved, turned)
    turned = jnp.where(col < rope_width, turned, 0.0)
    local = jnp.concatenate([absorbed, turned], 1)[: tokens * heads]
    out_ref[...] = jnp.broadcast_to(local[None], out_ref.shape).astype(BF16)


def merge(blocks):
    return jnp.concatenate([blocks[i] for i in range(blocks.shape[0])], 0)


def spread_kernel(query_ref, out_ref):
    rows = merge(query_ref[...].astype(F32)).astype(BF16)
    for i in range(out_ref.shape[0]):
        out_ref[i] = rows


def with_stats(peak, total):
    lane = lax.broadcasted_iota(jnp.int32, peak.shape[:-1] + (128,), peak.ndim - 1)
    stats = jnp.zeros(lane.shape, F32)
    for i, term in enumerate(split3(peak) + split3(total)):
        stats = jnp.where(lane == i, term, stats)
    return stats


def combined(latent, sums_ref):
    stats = sums_ref[:, :, latent:].astype(F32)
    peak = stats[:, :, 0:1] + stats[:, :, 1:2] + stats[:, :, 2:3]
    total = stats[:, :, 3:4] + stats[:, :, 4:5] + stats[:, :, 5:6]
    top = jnp.max(peak, axis=0)
    factor = jnp.exp(peak - top[None])
    total = jnp.sum(factor * total, axis=0)
    summed = jnp.sum(factor * sums_ref[:, :, :latent].astype(F32), axis=0)
    return summed, top, total


def attend_kernel(heads, tokens, scale, latent, query_ref, cache_ref, length_ref, out_ref):
    rows = query_ref.shape[0]
    width, block_len = cache_ref.shape
    scores = jnp.dot(query_ref[:, :latent], cache_ref[:latent], preferred_element_type=F32)
    scores += jnp.dot(query_ref[:, latent:width], cache_ref[latent:], preferred_element_type=F32)
    scores = scores * scale
    block = lax.axis_index("z") * lax.axis_size("y") + lax.axis_index("y")
    limit = length_ref[0] - tokens + 1 - block * block_len
    row = lax.broadcasted_iota(jnp.int32, (rows, 1), 0)
    limits = limit + (row // heads) % tokens
    visible = lax.broadcasted_iota(jnp.int32, (rows, block_len), 1) < limits
    scores = jnp.where(visible, scores, HIDDEN)
    peak = jnp.max(scores, axis=1, keepdims=True)
    weights = jnp.where(visible, jnp.exp(scores - peak), 0.0)
    total = jnp.sum(weights, axis=1, keepdims=True)
    summed = lax.dot_general(
        weights.astype(BF16),
        cache_ref[:latent],
        (((1,), (1,)), ((), ())),
        preferred_element_type=F32,
    )
    out_ref[:, :latent] = summed.astype(BF16)
    out_ref[:, latent:] = with_stats(peak, total).astype(BF16)


def add_kernel(latent, sums_ref, out_ref):
    summed, top, total = combined(latent, sums_ref)
    out = jnp.concatenate([summed, with_stats(top, total)], 1)
    rows = out_ref.shape[1]
    for i in range(out_ref.shape[0]):
        out_ref[i] = out[i * rows : (i + 1) * rows].astype(BF16)


def combine_kernel(heads, tokens, latent, sums_ref, parts_ref, out_ref):
    summed, _, total = combined(latent, sums_ref)
    mixed = (summed / total).astype(BF16)
    groups, rows = parts_ref.shape[0], parts_ref.shape[1]
    depth = latent // groups
    first = rows - heads * depth
    values = jnp.concatenate(
        [
            parts_ref[:, first + h * depth : first + (h + 1) * depth, :].reshape(latent, 128)
            for h in range(heads)
        ],
        1,
    )
    out = jnp.dot(mixed, values, preferred_element_type=F32)
    for t in range(tokens):
        for h in range(heads):
            out_ref[0, t : t + 1, h * 128 : (h + 1) * 128] = out[
                t * heads + h : t * heads + h + 1, h * 128 : (h + 1) * 128
            ].astype(BF16)


def call(kernel, shape, count, specs=None):
    return pl.pallas_call(
        kernel,
        out_shape=jax.ShapeDtypeStruct(shape, BF16),
        in_specs=specs or [VMEM] * count,
        out_specs=VMEM,
        compiler_params=PARAMS,
    )


def body(sizes, query_nope, query_rope, latent_cache, lengths, key_up, value_up):
    heads, depth, latent = key_up.shape
    groups, high, low = sizes["batch"], sizes["z"], sizes["y"]
    tokens = query_nope.shape[1]
    head_width = query_nope.shape[2] // heads
    rope_width = query_rope.shape[2] // heads
    own = tokens * heads
    wide = latent + 128
    part_rows = (key_up.size + value_up.size) // 128
    copies = call(pack_kernel, (groups, part_rows, 128), 2)(key_up, value_up)
    parts = lax.all_to_all(copies, "batch", 0, 0, tiled=True)
    absorb = functools.partial(absorb_kernel, heads, latent)
    queries = call(absorb, (high, own, wide), 3)(parts, query_nope, query_rope)
    queries = lax.all_to_all(queries, "z", 0, 0, tiled=True)
    queries = call(spread_kernel, (low, high * own, wide), 1)(queries)
    queries = lax.all_to_all(queries, "y", 0, 0, tiled=True)
    scale = 1.0 / math.sqrt(head_width + rope_width)
    attend = functools.partial(attend_kernel, heads, tokens, scale, latent)
    sums = call(attend, (low * high * own, wide), 3, [VMEM, VMEM, SMEM])(
        queries.reshape(low * high * own, wide), latent_cache[0].T, lengths
    )
    sums = lax.all_to_all(sums.reshape(low, high * own, wide), "y", 0, 0, tiled=True)
    sums = call(functools.partial(add_kernel, latent), (high, own, wide), 1)(sums)
    sums = lax.all_to_all(sums, "z", 0, 0, tiled=True)
    combine = functools.partial(combine_kernel, heads, tokens, latent)
    return call(combine, (1, tokens, heads * 128), 2)(sums, parts)


Y_SIZE = 4


def solution(mesh):
    batch, seq = mesh.shape["batch"], mesh.shape["seq"]
    mesh = Mesh(mesh.devices.reshape(batch, seq // Y_SIZE, Y_SIZE), ("batch", "z", "y"))
    both = ("z", "y")
    in_specs = (
        P("batch", None, both),
        P("batch", None, both),
        P("batch", both, None),
        P("batch"),
        P(both, "batch", None),
        P(both, "batch", None),
    )
    out_specs = P("batch", None, both)
    run = functools.partial(body, dict(mesh.shape))
    return jax.shard_map(run, mesh=mesh, in_specs=in_specs, out_specs=out_specs, check_vma=False)
```

```python
import functools
import math

import jax
import jax.numpy as jnp
from jax import lax
from jax.experimental import pallas as pl
from jax.experimental.pallas import tpu as pltpu
from jax.sharding import Mesh
from jax.sharding import PartitionSpec as P

VMEM = pl.BlockSpec(memory_space=pltpu.VMEM)
PARAMS = pltpu.CompilerParams(vmem_limit_bytes=24 * 1024 * 1024)
F32 = jnp.float32
BF16 = jnp.bfloat16
HIDDEN = -1e30
LOG2_E = math.log2(math.e)


def split3(x):
    high = x.astype(BF16).astype(F32)
    rest = x - high
    mid = rest.astype(BF16).astype(F32)
    return high, mid, (rest - mid).astype(BF16).astype(F32)


def pack_kernel(
    key_ref, value_ref, nope_ref, rope_ref, out_ref, nope_out, rope_out, key, value, sems
):
    pairs = (
        (key_ref, key),
        (value_ref, value),
        (nope_ref, nope_out),
        (rope_ref, rope_out),
    )
    copies = [
        pltpu.make_async_copy(source, target, sems.at[i])
        for i, (source, target) in enumerate(pairs)
    ]
    for copy in copies:
        copy.start()
    for copy in copies:
        copy.wait()
    heads, depth, latent = key.shape
    rows = [key[:, :, c : c + 128].reshape(heads * depth, 128) for c in range(0, latent, 128)]
    both = jnp.concatenate(rows + [value[...].reshape(-1, 128)], 0)
    for i in range(out_ref.shape[0]):
        out_ref[i] = both


def absorb_kernel(heads, latent, parts_ref, nope_ref, rope_ref, out_ref):
    tokens = nope_ref.shape[1]
    head_width = nope_ref.shape[2] // heads
    rope_width = rope_ref.shape[2] // heads
    groups = parts_ref.shape[0]
    depth = head_width // groups
    blocks = []
    for c in range(latent // 128):
        rows = [
            parts_ref[:, (c * heads + h) * depth : (c * heads + h + 1) * depth, :].reshape(
                head_width, 128
            )
            for h in range(heads)
        ]
        blocks.append(jnp.concatenate(rows, 0))
    keys = jnp.concatenate(blocks, 1)
    row = lax.broadcasted_iota(jnp.int32, (8, heads * head_width), 0)
    col = lax.broadcasted_iota(jnp.int32, (8, heads * head_width), 1)
    nope = nope_ref[0].astype(F32)
    spread = jnp.zeros(row.shape, F32)
    for t in range(tokens):
        spread = jnp.where(row // heads == t, nope[t : t + 1], spread)
    spread = jnp.where(row % heads == col // head_width, spread, 0.0)
    absorbed = jnp.dot(spread.astype(BF16), keys, preferred_element_type=F32)
    rope = rope_ref[0].astype(F32)
    row = lax.broadcasted_iota(jnp.int32, (8, 128), 0)
    col = lax.broadcasted_iota(jnp.int32, (8, 128), 1)
    turned = jnp.zeros(row.shape, F32)
    for t in range(tokens):
        for h in range(heads):
            moved = rope[t : t + 1]
            if h:
                moved = pltpu.roll(moved, 128 - h * rope_width, 1)
            turned = jnp.where(row == t * heads + h, moved, turned)
    turned = jnp.where(col < rope_width, turned, 0.0)
    local = jnp.concatenate([absorbed, turned], 1)[: tokens * heads]
    out_ref[...] = jnp.broadcast_to(local[None], out_ref.shape).astype(BF16)


def with_stats(peak, total):
    lane = lax.broadcasted_iota(jnp.int32, peak.shape[:-1] + (128,), peak.ndim - 1)
    stats = jnp.zeros(lane.shape, F32)
    for i, term in enumerate(split3(peak) + split3(total)):
        stats = jnp.where(lane == i, term, stats)
    return stats


def combined(latent, sums_ref):
    stats = sums_ref[:, :, latent:].astype(F32)
    peak = stats[:, :, 0:1] + stats[:, :, 1:2] + stats[:, :, 2:3]
    total = stats[:, :, 3:4] + stats[:, :, 4:5] + stats[:, :, 5:6]
    top = jnp.max(peak, axis=0)
    factor = jnp.exp(peak - top[None])
    total = jnp.sum(factor * total, axis=0)
    summed = jnp.sum(factor * sums_ref[:, :, :latent].astype(F32), axis=0)
    return summed, top, total


def attend_kernel(heads, tokens, scale, latent, query_ref, cache_ref, length_ref, out_ref):
    rows = query_ref.shape[0]
    width, block_len = cache_ref.shape
    scores = jnp.dot(query_ref[:, :latent], cache_ref[:latent], preferred_element_type=F32)
    scores += jnp.dot(query_ref[:, latent:width], cache_ref[latent:], preferred_element_type=F32)
    block = lax.axis_index("z") * lax.axis_size("y") + lax.axis_index("y")
    limit = length_ref[0] - tokens + 1 - block * block_len
    row = lax.broadcasted_iota(jnp.int32, (rows, 1), 0)
    limits = limit + (row // heads) % tokens
    visible = lax.broadcasted_iota(jnp.int32, (rows, block_len), 1) < limits
    scores = jnp.where(visible, scores, HIDDEN)
    peak = jnp.maximum(jnp.max(scores, axis=1, keepdims=True), HIDDEN / 2)
    weights = jnp.exp2((scores - peak) * (scale * LOG2_E))
    total = jnp.sum(weights, axis=1, keepdims=True)
    peak = peak * scale
    summed = lax.dot_general(
        weights.astype(BF16),
        cache_ref[:latent],
        (((1,), (1,)), ((), ())),
        preferred_element_type=F32,
    )
    out_ref[:, :latent] = summed.astype(BF16)
    out_ref[:, latent:] = with_stats(peak, total).astype(BF16)


def add_kernel(latent, sums_ref, out_ref):
    summed, top, total = combined(latent, sums_ref)
    out = jnp.concatenate([summed, with_stats(top, total)], 1)
    rows = out_ref.shape[1]
    for i in range(out_ref.shape[0]):
        out_ref[i] = out[i * rows : (i + 1) * rows].astype(BF16)


def combine_kernel(heads, tokens, latent, sums_ref, parts_ref, out_ref):
    summed, _, total = combined(latent, sums_ref)
    mixed = (summed / total).astype(BF16)
    groups, rows = parts_ref.shape[0], parts_ref.shape[1]
    depth = latent // groups
    first = rows - heads * depth
    values = jnp.concatenate(
        [
            parts_ref[:, first + h * depth : first + (h + 1) * depth, :].reshape(latent, 128)
            for h in range(heads)
        ],
        1,
    )
    out = jnp.dot(mixed, values, preferred_element_type=F32)
    for t in range(tokens):
        for h in range(heads):
            out_ref[0, t : t + 1, h * 128 : (h + 1) * 128] = out[
                t * heads + h : t * heads + h + 1, h * 128 : (h + 1) * 128
            ].astype(BF16)


def call(kernel, shape, count, specs=None):
    return pl.pallas_call(
        kernel,
        out_shape=jax.ShapeDtypeStruct(shape, BF16),
        in_specs=specs or [VMEM] * count,
        out_specs=VMEM,
        compiler_params=PARAMS,
    )


def body(sizes, query_nope, query_rope, latent_cache, lengths, key_up, value_up):
    heads, depth, latent = key_up.shape
    groups, high, low = sizes["batch"], sizes["z"], sizes["y"]
    tokens = query_nope.shape[1]
    head_width = query_nope.shape[2] // heads
    rope_width = query_rope.shape[2] // heads
    own = tokens * heads
    wide = latent + 128
    part_rows = (key_up.size + value_up.size) // 128
    like = jax.ShapeDtypeStruct
    copies, nope, rope = pl.pallas_call(
        pack_kernel,
        out_shape=(
            like((groups, part_rows, 128), BF16),
            like(query_nope.shape, BF16),
            like(query_rope.shape, BF16),
        ),
        in_specs=[pl.BlockSpec(memory_space=pl.ANY)] * 4,
        out_specs=[VMEM] * 3,
        scratch_shapes=[
            pltpu.VMEM(key_up.shape, BF16),
            pltpu.VMEM(value_up.shape, BF16),
            pltpu.SemaphoreType.DMA((4,)),
        ],
        compiler_params=PARAMS,
    )(*[
        pltpu.with_memory_space_constraint(array, pltpu.HBM)
        for array in (key_up, value_up, query_nope, query_rope)
    ])
    parts = lax.all_to_all(copies, "batch", 0, 0, tiled=True)
    absorb = functools.partial(absorb_kernel, heads, latent)
    queries = call(absorb, (high, own, wide), 3)(parts, nope, rope)
    queries = lax.all_to_all(queries, "z", 0, 0, tiled=True)
    queries = jnp.broadcast_to(queries.reshape(high * own, wide), (low, high * own, wide))
    queries = lax.all_to_all(queries, "y", 0, 0, tiled=True)
    scale = 1.0 / math.sqrt(head_width + rope_width)
    attend = functools.partial(attend_kernel, heads, tokens, scale, latent)
    sums = call(attend, (low * high * own, wide), 3, [VMEM, VMEM, pl.BlockSpec(memory_space=pltpu.SMEM)])(
        queries.reshape(low * high * own, wide), latent_cache[0].T, lengths
    )
    sums = lax.all_to_all(sums.reshape(low, high * own, wide), "y", 0, 0, tiled=True)
    sums = call(functools.partial(add_kernel, latent), (high, own, wide), 1)(sums)
    sums = lax.all_to_all(sums, "z", 0, 0, tiled=True)
    combine = functools.partial(combine_kernel, heads, tokens, latent)
    return call(combine, (1, tokens, heads * 128), 2)(sums, parts)


Y_SIZE = 4


def solution(mesh):
    batch, seq = mesh.shape["batch"], mesh.shape["seq"]
    mesh = Mesh(mesh.devices.reshape(batch, seq // Y_SIZE, Y_SIZE), ("batch", "z", "y"))
    both = ("z", "y")
    in_specs = (
        P("batch", None, both),
        P("batch", None, both),
        P("batch", both, None),
        P("batch"),
        P(both, "batch", None),
        P(both, "batch", None),
    )
    out_specs = P("batch", None, both)
    run = functools.partial(body, dict(mesh.shape))
    return jax.shard_map(run, mesh=mesh, in_specs=in_specs, out_specs=out_specs, check_vma=False)
```

```python
import functools
import math

import jax
import jax.numpy as jnp
from jax import lax
from jax.experimental import pallas as pl
from jax.experimental.pallas import tpu as pltpu
from jax.sharding import Mesh
from jax.sharding import PartitionSpec as P

VMEM = pl.BlockSpec(memory_space=pltpu.VMEM)
PARAMS = pltpu.CompilerParams(vmem_limit_bytes=24 * 1024 * 1024)
F32 = jnp.float32
BF16 = jnp.bfloat16
HIDDEN = -1e30
LOG2_E = math.log2(math.e)


def split3(x):
    high = x.astype(BF16).astype(F32)
    rest = x - high
    mid = rest.astype(BF16).astype(F32)
    return high, mid, (rest - mid).astype(BF16).astype(F32)


def places(groups):
    return [(i - FIRST["batch"]) % groups for i in range(groups)]


def pack_kernel(
    key_ref, value_ref, nope_ref, rope_ref, out_ref, nope_out, rope_out, key, value, sems
):
    pairs = (
        (key_ref, key),
        (value_ref, value),
        (nope_ref, nope_out),
        (rope_ref, rope_out),
    )
    copies = [
        pltpu.make_async_copy(source, target, sems.at[i])
        for i, (source, target) in enumerate(pairs)
    ]
    for copy in copies:
        copy.start()
    for copy in copies:
        copy.wait()
    heads, depth, latent = key.shape
    rows = [key[:, :, c : c + 128].reshape(heads * depth, 128) for c in range(0, latent, 128)]
    both = jnp.concatenate(rows + [value[...].reshape(-1, 128)], 0)
    for i in range(out_ref.shape[0]):
        out_ref[i] = both


def absorb_kernel(heads, latent, parts_ref, nope_ref, rope_ref, out_ref):
    tokens = nope_ref.shape[1]
    head_width = nope_ref.shape[2] // heads
    rope_width = rope_ref.shape[2] // heads
    groups = parts_ref.shape[0]
    depth = head_width // groups
    blocks = []
    for c in range(latent // 128):
        rows = [
            parts_ref[place, (c * heads + h) * depth : (c * heads + h + 1) * depth]
            for h in range(heads)
            for place in places(groups)
        ]
        blocks.append(jnp.concatenate(rows, 0))
    keys = jnp.concatenate(blocks, 1)
    row = lax.broadcasted_iota(jnp.int32, (8, heads * head_width), 0)
    col = lax.broadcasted_iota(jnp.int32, (8, heads * head_width), 1)
    nope = nope_ref[0].astype(F32)
    spread = jnp.zeros(row.shape, F32)
    for t in range(tokens):
        spread = jnp.where(row // heads == t, nope[t : t + 1], spread)
    spread = jnp.where(row % heads == col // head_width, spread, 0.0)
    absorbed = jnp.dot(spread.astype(BF16), keys, preferred_element_type=F32)
    rope = rope_ref[0].astype(F32)
    row = lax.broadcasted_iota(jnp.int32, (8, 128), 0)
    col = lax.broadcasted_iota(jnp.int32, (8, 128), 1)
    turned = jnp.zeros(row.shape, F32)
    for t in range(tokens):
        for h in range(heads):
            moved = rope[t : t + 1]
            if h:
                moved = pltpu.roll(moved, 128 - h * rope_width, 1)
            turned = jnp.where(row == t * heads + h, moved, turned)
    turned = jnp.where(col < rope_width, turned, 0.0)
    local = jnp.concatenate([absorbed, turned], 1)[: tokens * heads]
    out_ref[...] = jnp.broadcast_to(local[None], out_ref.shape).astype(BF16)


def with_stats(peak, total):
    lane = lax.broadcasted_iota(jnp.int32, peak.shape[:-1] + (128,), peak.ndim - 1)
    stats = jnp.zeros(lane.shape, F32)
    for i, term in enumerate(split3(peak) + split3(total)):
        stats = jnp.where(lane == i, term, stats)
    return stats


def combined(latent, sums_ref):
    stats = sums_ref[:, :, latent:].astype(F32)
    peak = stats[:, :, 0:1] + stats[:, :, 1:2] + stats[:, :, 2:3]
    total = stats[:, :, 3:4] + stats[:, :, 4:5] + stats[:, :, 5:6]
    top = jnp.max(peak, axis=0)
    factor = jnp.exp(peak - top[None])
    total = jnp.sum(factor * total, axis=0)
    summed = jnp.sum(factor * sums_ref[:, :, :latent].astype(F32), axis=0)
    return summed, top, total


def attend_kernel(heads, tokens, scale, latent, query_ref, cache_ref, length_ref, out_ref):
    rows = query_ref.shape[0]
    width, block_len = cache_ref.shape
    scores = jnp.dot(query_ref[:, :latent], cache_ref[:latent], preferred_element_type=F32)
    scores += jnp.dot(query_ref[:, latent:width], cache_ref[latent:], preferred_element_type=F32)
    block = lax.axis_index("z") * lax.axis_size("y") + lax.axis_index("y")
    limit = length_ref[0] - tokens + 1 - block * block_len
    row = lax.broadcasted_iota(jnp.int32, (rows, 1), 0)
    limits = limit + (row // heads) % tokens
    visible = lax.broadcasted_iota(jnp.int32, (rows, block_len), 1) < limits
    scores = jnp.where(visible, scores, HIDDEN)
    peak = jnp.maximum(jnp.max(scores, axis=1, keepdims=True), HIDDEN / 2)
    weights = jnp.exp2((scores - peak) * (scale * LOG2_E))
    total = jnp.sum(weights, axis=1, keepdims=True)
    peak = peak * scale
    summed = lax.dot_general(
        weights.astype(BF16),
        cache_ref[:latent],
        (((1,), (1,)), ((), ())),
        preferred_element_type=F32,
    )
    out_ref[:, :latent] = summed.astype(BF16)
    out_ref[:, latent:] = with_stats(peak, total).astype(BF16)


def add_kernel(latent, sums_ref, out_ref):
    summed, top, total = combined(latent, sums_ref)
    out = jnp.concatenate([summed, with_stats(top, total)], 1)
    rows = out_ref.shape[1]
    for i in range(out_ref.shape[0]):
        out_ref[i] = out[i * rows : (i + 1) * rows].astype(BF16)


def combine_kernel(heads, tokens, latent, sums_ref, parts_ref, out_ref):
    summed, _, total = combined(latent, sums_ref)
    mixed = (summed / total).astype(BF16)
    groups, rows = parts_ref.shape[0], parts_ref.shape[1]
    depth = latent // groups
    first = rows - heads * depth
    values = jnp.concatenate(
        [
            jnp.concatenate(
                [
                    parts_ref[place, first + h * depth : first + (h + 1) * depth]
                    for place in places(groups)
                ],
                0,
            )
            for h in range(heads)
        ],
        1,
    )
    out = jnp.dot(mixed, values, preferred_element_type=F32)
    for t in range(tokens):
        for h in range(heads):
            out_ref[0, t : t + 1, h * 128 : (h + 1) * 128] = out[
                t * heads + h : t * heads + h + 1, h * 128 : (h + 1) * 128
            ].astype(BF16)


def call(kernel, shape, count, specs=None):
    return pl.pallas_call(
        kernel,
        out_shape=jax.ShapeDtypeStruct(shape, BF16),
        in_specs=specs or [VMEM] * count,
        out_specs=VMEM,
        compiler_params=PARAMS,
    )


FIRST = {"batch": 5, "z": 8, "y": 2}


def order(axis, size):
    return [(i + FIRST[axis]) % size for i in range(size)]


def exchange(blocks, axis):
    groups = [order(axis, blocks.shape[0])]
    return lax.all_to_all(blocks, axis, 0, 0, axis_index_groups=groups, tiled=True)


def body(sizes, query_nope, query_rope, latent_cache, lengths, key_up, value_up):
    heads, depth, latent = key_up.shape
    groups, high, low = sizes["batch"], sizes["z"], sizes["y"]
    tokens = query_nope.shape[1]
    head_width = query_nope.shape[2] // heads
    rope_width = query_rope.shape[2] // heads
    own = tokens * heads
    wide = latent + 128
    part_rows = (key_up.size + value_up.size) // 128
    like = jax.ShapeDtypeStruct
    copies, nope, rope = pl.pallas_call(
        pack_kernel,
        out_shape=(
            like((groups, part_rows, 128), BF16),
            like(query_nope.shape, BF16),
            like(query_rope.shape, BF16),
        ),
        in_specs=[pl.BlockSpec(memory_space=pl.ANY)] * 4,
        out_specs=[VMEM] * 3,
        scratch_shapes=[
            pltpu.VMEM(key_up.shape, BF16),
            pltpu.VMEM(value_up.shape, BF16),
            pltpu.SemaphoreType.DMA((4,)),
        ],
        compiler_params=PARAMS,
    )(*[
        pltpu.with_memory_space_constraint(array, pltpu.HBM)
        for array in (key_up, value_up, query_nope, query_rope)
    ])
    parts = exchange(copies, "batch")
    absorb = functools.partial(absorb_kernel, heads, latent)
    queries = call(absorb, (high, own, wide), 3)(parts, nope, rope)
    queries = exchange(queries, "z")
    queries = jnp.broadcast_to(queries.reshape(high * own, wide), (low, high * own, wide))
    queries = exchange(queries, "y")
    scale = 1.0 / math.sqrt(head_width + rope_width)
    attend = functools.partial(attend_kernel, heads, tokens, scale, latent)
    sums = call(attend, (low * high * own, wide), 3, [VMEM, VMEM, pl.BlockSpec(memory_space=pltpu.SMEM)])(
        queries.reshape(low * high * own, wide), latent_cache[0].T, lengths
    )
    sums = exchange(sums.reshape(low, high * own, wide), "y")
    sums = call(functools.partial(add_kernel, latent), (high, own, wide), 1)(sums)
    sums = exchange(sums, "z")
    combine = functools.partial(combine_kernel, heads, tokens, latent)
    return call(combine, (1, tokens, heads * 128), 2)(sums, parts)


Y_SIZE = 4


def solution(mesh):
    batch, seq = mesh.shape["batch"], mesh.shape["seq"]
    mesh = Mesh(mesh.devices.reshape(batch, seq // Y_SIZE, Y_SIZE), ("batch", "z", "y"))
    both = ("z", "y")
    in_specs = (
        P("batch", None, both),
        P("batch", None, both),
        P("batch", both, None),
        P("batch"),
        P(both, "batch", None),
        P(both, "batch", None),
    )
    out_specs = P("batch", None, both)
    run = functools.partial(body, dict(mesh.shape))
    return jax.shard_map(run, mesh=mesh, in_specs=in_specs, out_specs=out_specs, check_vma=False)
```

```python
import functools
import math

import jax
import jax.numpy as jnp
from jax import lax
from jax.experimental import pallas as pl
from jax.experimental.pallas import tpu as pltpu
from jax.sharding import Mesh
from jax.sharding import PartitionSpec as P

VMEM = pl.BlockSpec(memory_space=pltpu.VMEM)
PARAMS = pltpu.CompilerParams(vmem_limit_bytes=24 * 1024 * 1024)
F32 = jnp.float32
BF16 = jnp.bfloat16
HIDDEN = -1e30
LOG2_E = math.log2(math.e)


def split3(x):
    high = x.astype(BF16).astype(F32)
    rest = x - high
    mid = rest.astype(BF16).astype(F32)
    return high, mid, (rest - mid).astype(BF16).astype(F32)


def places(groups):
    return [(i - FIRST["batch"]) % groups for i in range(groups)]


def pack_kernel(
    key_ref, value_ref, nope_ref, rope_ref, out_ref, nope_out, rope_out, key, value, sems
):
    pairs = (
        (key_ref, key),
        (value_ref, value),
        (nope_ref, nope_out),
        (rope_ref, rope_out),
    )
    copies = [
        pltpu.make_async_copy(source, target, sems.at[i])
        for i, (source, target) in enumerate(pairs)
    ]
    for copy in copies:
        copy.start()
    for copy in copies:
        copy.wait()
    heads, depth, latent = key.shape
    rows = [key[:, :, c : c + 128].reshape(heads * depth, 128) for c in range(0, latent, 128)]
    keys = jnp.concatenate(rows, 0)
    for i, member in enumerate(order("batch", out_ref.shape[0])):
        out_ref[i] = jnp.concatenate([keys, value[member % heads]], 0)


def absorb_kernel(heads, latent, parts_ref, nope_ref, rope_ref, out_ref, values_ref):
    values_ref[...] = parts_ref[:, parts_ref.shape[1] - values_ref.shape[1] :]
    tokens = nope_ref.shape[1]
    head_width = nope_ref.shape[2] // heads
    rope_width = rope_ref.shape[2] // heads
    groups = parts_ref.shape[0]
    depth = head_width // groups
    blocks = []
    for c in range(latent // 128):
        rows = [
            parts_ref[place, (c * heads + h) * depth : (c * heads + h + 1) * depth]
            for h in range(heads)
            for place in places(groups)
        ]
        blocks.append(jnp.concatenate(rows, 0))
    keys = jnp.concatenate(blocks, 1)
    row = lax.broadcasted_iota(jnp.int32, (8, heads * head_width), 0)
    col = lax.broadcasted_iota(jnp.int32, (8, heads * head_width), 1)
    nope = nope_ref[0].astype(F32)
    spread = jnp.zeros(row.shape, F32)
    for t in range(tokens):
        spread = jnp.where(row // heads == t, nope[t : t + 1], spread)
    spread = jnp.where(row % heads == col // head_width, spread, 0.0)
    absorbed = jnp.dot(spread.astype(BF16), keys, preferred_element_type=F32)
    rope = rope_ref[0].astype(F32)
    row = lax.broadcasted_iota(jnp.int32, (8, 128), 0)
    col = lax.broadcasted_iota(jnp.int32, (8, 128), 1)
    turned = jnp.zeros(row.shape, F32)
    for t in range(tokens):
        for h in range(heads):
            moved = rope[t : t + 1]
            if h:
                moved = pltpu.roll(moved, 128 - h * rope_width, 1)
            turned = jnp.where(row == t * heads + h, moved, turned)
    turned = jnp.where(col < rope_width, turned, 0.0)
    local = jnp.concatenate([absorbed, turned], 1)[: tokens * heads]
    out_ref[...] = jnp.broadcast_to(local[None], out_ref.shape).astype(BF16)


def with_stats(peak, total):
    lane = lax.broadcasted_iota(jnp.int32, peak.shape[:-1] + (128,), peak.ndim - 1)
    stats = jnp.zeros(lane.shape, F32)
    for i, term in enumerate(split3(peak) + split3(total)):
        stats = jnp.where(lane == i, term, stats)
    return stats


def combined(latent, sums_ref):
    stats = sums_ref[:, :, latent:].astype(F32)
    lane = lax.broadcasted_iota(jnp.int32, stats.shape, 2)
    peak = jnp.sum(jnp.where(lane < 3, stats, 0.0), axis=2, keepdims=True)
    total = jnp.sum(jnp.where(lane < 3, 0.0, stats), axis=2, keepdims=True)
    top = jnp.max(peak, axis=0)
    factor = jnp.exp(peak - top[None])
    total = jnp.sum(factor * total, axis=0)
    summed = jnp.sum(factor * sums_ref[:, :, :latent].astype(F32), axis=0)
    return summed, top, total


def attend_kernel(heads, tokens, scale, latent, query_ref, cache_ref, length_ref, out_ref):
    rows = query_ref.shape[0]
    width, block_len = cache_ref.shape
    scores = jnp.dot(query_ref[:, :latent], cache_ref[:latent], preferred_element_type=F32)
    scores += jnp.dot(query_ref[:, latent:width], cache_ref[latent:], preferred_element_type=F32)
    block = lax.axis_index("z") * lax.axis_size("y") + lax.axis_index("y")
    limit = length_ref[0] - tokens + 1 - block * block_len
    row = lax.broadcasted_iota(jnp.int32, (rows, 1), 0)
    limits = limit + (row // heads) % tokens
    visible = lax.broadcasted_iota(jnp.int32, (rows, block_len), 1) < limits
    scores = jnp.where(visible, scores, HIDDEN)
    peak = jnp.maximum(jnp.max(scores, axis=1, keepdims=True), HIDDEN / 2)
    weights = jnp.exp2((scores - peak) * (scale * LOG2_E))
    total = jnp.sum(weights, axis=1, keepdims=True)
    peak = peak * scale
    summed = lax.dot_general(
        weights.astype(BF16),
        cache_ref[:latent],
        (((1,), (1,)), ((), ())),
        preferred_element_type=F32,
    )
    out_ref[:, :latent] = summed.astype(BF16)
    out_ref[:, latent:] = with_stats(peak, total).astype(BF16)


def add_kernel(latent, sums_ref, out_ref):
    summed, top, total = combined(latent, sums_ref)
    out = jnp.concatenate([summed, with_stats(top, total)], 1)
    rows = out_ref.shape[1]
    for i in range(out_ref.shape[0]):
        out_ref[i] = out[i * rows : (i + 1) * rows].astype(BF16)


def combine_kernel(heads, tokens, latent, sums_ref, own_ref, other_ref, out_ref):
    summed, _, total = combined(latent, sums_ref)
    mixed = (summed / total).astype(BF16)
    groups = own_ref.shape[0]
    own = jnp.concatenate([own_ref[place] for place in places(groups)], 0)
    other = jnp.concatenate([other_ref[place] for place in places(groups)], 0)
    second = lax.axis_index("batch") % 2 == 1
    values = jnp.concatenate([jnp.where(second, other, own), jnp.where(second, own, other)], 1)
    out = jnp.dot(mixed, values, preferred_element_type=F32)
    for t in range(tokens):
        for h in range(heads):
            out_ref[0, t : t + 1, h * 128 : (h + 1) * 128] = out[
                t * heads + h : t * heads + h + 1, h * 128 : (h + 1) * 128
            ].astype(BF16)


def call(kernel, shape, count, specs=None):
    return pl.pallas_call(
        kernel,
        out_shape=jax.ShapeDtypeStruct(shape, BF16),
        in_specs=specs or [VMEM] * count,
        out_specs=VMEM,
        compiler_params=PARAMS,
    )


FIRST = {"batch": 5, "z": 8, "y": 2}


def order(axis, size):
    return [(i + FIRST[axis]) % size for i in range(size)]


def exchange(blocks, axis):
    groups = [order(axis, blocks.shape[0])]
    return lax.all_to_all(blocks, axis, 0, 0, axis_index_groups=groups, tiled=True)


def body(sizes, query_nope, query_rope, latent_cache, lengths, key_up, value_up):
    heads, depth, latent = key_up.shape
    groups, high, low = sizes["batch"], sizes["z"], sizes["y"]
    tokens = query_nope.shape[1]
    head_width = query_nope.shape[2] // heads
    rope_width = query_rope.shape[2] // heads
    own = tokens * heads
    wide = latent + 128
    part_rows = (key_up.size + value_up.size // heads) // 128
    like = jax.ShapeDtypeStruct
    copies, nope, rope = pl.pallas_call(
        pack_kernel,
        out_shape=(
            like((groups, part_rows, 128), BF16),
            like(query_nope.shape, BF16),
            like(query_rope.shape, BF16),
        ),
        in_specs=[pl.BlockSpec(memory_space=pl.ANY)] * 4,
        out_specs=[VMEM] * 3,
        scratch_shapes=[
            pltpu.VMEM(key_up.shape, BF16),
            pltpu.VMEM(value_up.shape, BF16),
            pltpu.SemaphoreType.DMA((4,)),
        ],
        compiler_params=PARAMS,
    )(*[
        pltpu.with_memory_space_constraint(array, pltpu.HBM)
        for array in (key_up, value_up, query_nope, query_rope)
    ])
    parts = exchange(copies, "batch")
    absorb = functools.partial(absorb_kernel, heads, latent)
    queries, values = pl.pallas_call(
        absorb,
        out_shape=(
            like((high, own, wide), BF16),
            like((groups, latent // groups, 128), BF16),
        ),
        in_specs=[VMEM] * 3,
        out_specs=[VMEM] * 2,
        compiler_params=PARAMS,
    )(parts, nope, rope)
    queries = exchange(queries, "z")
    values, queries = lax.optimization_barrier((values, queries))
    queries = jnp.broadcast_to(queries.reshape(high * own, wide), (low, high * own, wide))
    queries = exchange(queries, "y")
    other = lax.ppermute(values, "batch", [(i, i ^ 1) for i in range(groups)])
    other, queries = lax.optimization_barrier((other, queries))
    scale = 1.0 / math.sqrt(head_width + rope_width)
    attend = functools.partial(attend_kernel, heads, tokens, scale, latent)
    sums = call(attend, (low * high * own, wide), 3, [VMEM, VMEM, pl.BlockSpec(memory_space=pltpu.SMEM)])(
        queries.reshape(low * high * own, wide), latent_cache[0].T, lengths
    )
    sums = exchange(sums.reshape(low, high * own, wide), "y")
    sums = call(functools.partial(add_kernel, latent), (high, own, wide), 1)(sums)
    sums = exchange(sums, "z")
    combine = functools.partial(combine_kernel, heads, tokens, latent)
    return call(combine, (1, tokens, heads * 128), 3)(sums, values, other)


Y_SIZE = 4


def solution(mesh):
    batch, seq = mesh.shape["batch"], mesh.shape["seq"]
    mesh = Mesh(mesh.devices.reshape(batch, seq // Y_SIZE, Y_SIZE), ("batch", "z", "y"))
    both = ("z", "y")
    in_specs = (
        P("batch", None, both),
        P("batch", None, both),
        P("batch", both, None),
        P("batch"),
        P(both, "batch", None),
        P(both, "batch", None),
    )
    out_specs = P("batch", None, both)
    run = functools.partial(body, dict(mesh.shape))
    return jax.shard_map(run, mesh=mesh, in_specs=in_specs, out_specs=out_specs, check_vma=False)
```

```python
import functools
import math

import jax
import jax.numpy as jnp
from jax import lax
from jax.experimental import pallas as pl
from jax.experimental.pallas import tpu as pltpu
from jax.sharding import Mesh
from jax.sharding import PartitionSpec as P

VMEM = pl.BlockSpec(memory_space=pltpu.VMEM)
PARAMS = pltpu.CompilerParams(vmem_limit_bytes=24 * 1024 * 1024)
F32 = jnp.float32
BF16 = jnp.bfloat16
HIDDEN = -1e30
LOG2_E = math.log2(math.e)


def split3(x):
    high = x.astype(BF16).astype(F32)
    rest = x - high
    mid = rest.astype(BF16).astype(F32)
    return high, mid, (rest - mid).astype(BF16).astype(F32)


def places(groups):
    return [(i - FIRST["batch"]) % groups for i in range(groups)]


def pack_kernel(
    key_ref, value_ref, nope_ref, rope_ref, out_ref, nope_out, rope_out, key, value, sems
):
    pairs = (
        (key_ref, key),
        (value_ref, value),
        (nope_ref, nope_out),
        (rope_ref, rope_out),
    )
    copies = [
        pltpu.make_async_copy(source, target, sems.at[i])
        for i, (source, target) in enumerate(pairs)
    ]
    for copy in copies:
        copy.start()
    copies[0].wait()
    heads, depth, latent = key.shape
    rows = [key[:, :, c : c + 128].reshape(heads * depth, 128) for c in range(0, latent, 128)]
    keys = jnp.concatenate(rows, 0)
    members = order("batch", out_ref.shape[0])
    for i in range(len(members)):
        out_ref[i, : keys.shape[0]] = keys
    copies[1].wait()
    for i, member in enumerate(members):
        out_ref[i, keys.shape[0] :] = value[member % heads]
    for copy in copies[2:]:
        copy.wait()


def absorb_kernel(heads, latent, parts_ref, nope_ref, rope_ref, out_ref, values_ref):
    values_ref[...] = parts_ref[:, parts_ref.shape[1] - values_ref.shape[1] :]
    tokens = nope_ref.shape[1]
    head_width = nope_ref.shape[2] // heads
    rope_width = rope_ref.shape[2] // heads
    groups = parts_ref.shape[0]
    depth = head_width // groups
    blocks = []
    for c in range(latent // 128):
        rows = [
            parts_ref[place, (c * heads + h) * depth : (c * heads + h + 1) * depth]
            for h in range(heads)
            for place in places(groups)
        ]
        blocks.append(jnp.concatenate(rows, 0))
    keys = jnp.concatenate(blocks, 1)
    row = lax.broadcasted_iota(jnp.int32, (8, heads * head_width), 0)
    col = lax.broadcasted_iota(jnp.int32, (8, heads * head_width), 1)
    nope = nope_ref[0].astype(F32)
    spread = jnp.zeros(row.shape, F32)
    for t in range(tokens):
        spread = jnp.where(row // heads == t, nope[t : t + 1], spread)
    spread = jnp.where(row % heads == col // head_width, spread, 0.0)
    absorbed = jnp.dot(spread.astype(BF16), keys, preferred_element_type=F32)
    rope = rope_ref[0].astype(F32)
    row = lax.broadcasted_iota(jnp.int32, (8, 128), 0)
    col = lax.broadcasted_iota(jnp.int32, (8, 128), 1)
    turned = jnp.zeros(row.shape, F32)
    for t in range(tokens):
        for h in range(heads):
            moved = rope[t : t + 1]
            if h:
                moved = pltpu.roll(moved, 128 - h * rope_width, 1)
            turned = jnp.where(row == t * heads + h, moved, turned)
    turned = jnp.where(col < rope_width, turned, 0.0)
    local = jnp.concatenate([absorbed, turned], 1)[: tokens * heads]
    out_ref[...] = jnp.broadcast_to(local[None], out_ref.shape).astype(BF16)


def with_stats(peak, total):
    lane = lax.broadcasted_iota(jnp.int32, peak.shape[:-1] + (128,), peak.ndim - 1)
    stats = jnp.zeros(lane.shape, F32)
    for i, term in enumerate(split3(peak) + split3(total)):
        stats = jnp.where(lane == i, term, stats)
    return stats


def combined(latent, sums_ref):
    stats = sums_ref[:, :, latent:].astype(F32)
    lane = lax.broadcasted_iota(jnp.int32, stats.shape, 2)
    peak = jnp.sum(jnp.where(lane < 3, stats, 0.0), axis=2, keepdims=True)
    total = jnp.sum(jnp.where(lane < 3, 0.0, stats), axis=2, keepdims=True)
    top = jnp.max(peak, axis=0)
    factor = jnp.exp(peak - top[None])
    total = jnp.sum(factor * total, axis=0)
    summed = jnp.sum(factor * sums_ref[:, :, :latent].astype(F32), axis=0)
    return summed, top, total


def attend_kernel(heads, tokens, scale, latent, query_ref, cache_ref, length_ref, out_ref):
    rows = query_ref.shape[0]
    width, block_len = cache_ref.shape
    scores = jnp.dot(query_ref[:, :latent], cache_ref[:latent], preferred_element_type=F32)
    scores += jnp.dot(query_ref[:, latent:width], cache_ref[latent:], preferred_element_type=F32)
    block = lax.axis_index("z") * lax.axis_size("y") + lax.axis_index("y")
    limit = length_ref[0] - tokens + 1 - block * block_len
    row = lax.broadcasted_iota(jnp.int32, (rows, 1), 0)
    limits = limit + (row // heads) % tokens
    visible = lax.broadcasted_iota(jnp.int32, (rows, block_len), 1) < limits
    scores = jnp.where(visible, scores, HIDDEN)
    peak = jnp.maximum(jnp.max(scores, axis=1, keepdims=True), HIDDEN / 2)
    weights = jnp.exp2((scores - peak) * (scale * LOG2_E))
    total = jnp.sum(weights, axis=1, keepdims=True)
    peak = peak * scale
    summed = lax.dot_general(
        weights.astype(BF16),
        cache_ref[:latent],
        (((1,), (1,)), ((), ())),
        preferred_element_type=F32,
    )
    out_ref[:, :latent] = summed.astype(BF16)
    out_ref[:, latent:] = with_stats(peak, total).astype(BF16)


def add_kernel(latent, sums_ref, out_ref):
    summed, top, total = combined(latent, sums_ref)
    out = jnp.concatenate([summed, with_stats(top, total)], 1)
    rows = out_ref.shape[1]
    for i in range(out_ref.shape[0]):
        out_ref[i] = out[i * rows : (i + 1) * rows].astype(BF16)


def combine_kernel(heads, tokens, latent, sums_ref, own_ref, other_ref, out_ref):
    summed, _, total = combined(latent, sums_ref)
    mixed = (summed / total).astype(BF16)
    groups = own_ref.shape[0]
    own = jnp.concatenate([own_ref[place] for place in places(groups)], 0)
    other = jnp.concatenate([other_ref[place] for place in places(groups)], 0)
    second = lax.axis_index("batch") % 2 == 1
    values = jnp.concatenate([jnp.where(second, other, own), jnp.where(second, own, other)], 1)
    out = jnp.dot(mixed, values, preferred_element_type=F32)
    for t in range(tokens):
        for h in range(heads):
            out_ref[0, t : t + 1, h * 128 : (h + 1) * 128] = out[
                t * heads + h : t * heads + h + 1, h * 128 : (h + 1) * 128
            ].astype(BF16)


def call(kernel, shape, count, specs=None):
    return pl.pallas_call(
        kernel,
        out_shape=jax.ShapeDtypeStruct(shape, BF16),
        in_specs=specs or [VMEM] * count,
        out_specs=VMEM,
        compiler_params=PARAMS,
    )


FIRST = {"batch": 5, "z": 8, "y": 2}


def order(axis, size):
    return [(i + FIRST[axis]) % size for i in range(size)]


def exchange(blocks, axis):
    groups = [order(axis, blocks.shape[0])]
    return lax.all_to_all(blocks, axis, 0, 0, axis_index_groups=groups, tiled=True)


def body(sizes, query_nope, query_rope, latent_cache, lengths, key_up, value_up):
    heads, depth, latent = key_up.shape
    groups, high, low = sizes["batch"], sizes["z"], sizes["y"]
    tokens = query_nope.shape[1]
    head_width = query_nope.shape[2] // heads
    rope_width = query_rope.shape[2] // heads
    own = tokens * heads
    wide = latent + 128
    part_rows = (key_up.size + value_up.size // heads) // 128
    like = jax.ShapeDtypeStruct
    copies, nope, rope = pl.pallas_call(
        pack_kernel,
        out_shape=(
            like((groups, part_rows, 128), BF16),
            like(query_nope.shape, BF16),
            like(query_rope.shape, BF16),
        ),
        in_specs=[pl.BlockSpec(memory_space=pl.ANY)] * 4,
        out_specs=[VMEM] * 3,
        scratch_shapes=[
            pltpu.VMEM(key_up.shape, BF16),
            pltpu.VMEM(value_up.shape, BF16),
            pltpu.SemaphoreType.DMA((4,)),
        ],
        compiler_params=PARAMS,
    )(*[
        pltpu.with_memory_space_constraint(array, pltpu.HBM)
        for array in (key_up, value_up, query_nope, query_rope)
    ])
    parts = exchange(copies, "batch")
    absorb = functools.partial(absorb_kernel, heads, latent)
    queries, values = pl.pallas_call(
        absorb,
        out_shape=(
            like((high, own, wide), BF16),
            like((groups, latent // groups, 128), BF16),
        ),
        in_specs=[VMEM] * 3,
        out_specs=[VMEM] * 2,
        compiler_params=PARAMS,
    )(parts, nope, rope)
    queries = exchange(queries, "z")
    values, queries = lax.optimization_barrier((values, queries))
    queries = jnp.broadcast_to(queries.reshape(high * own, wide), (low, high * own, wide))
    queries = exchange(queries, "y")
    other = lax.ppermute(values, "batch", [(i, i ^ 1) for i in range(groups)])
    other, queries = lax.optimization_barrier((other, queries))
    scale = 1.0 / math.sqrt(head_width + rope_width)
    attend = functools.partial(attend_kernel, heads, tokens, scale, latent)
    sums = call(attend, (low * high * own, wide), 3, [VMEM, VMEM, pl.BlockSpec(memory_space=pltpu.SMEM)])(
        queries.reshape(low * high * own, wide), latent_cache[0].T, lengths
    )
    sums = exchange(sums.reshape(low, high * own, wide), "y")
    sums = call(functools.partial(add_kernel, latent), (high, own, wide), 1)(sums)
    sums = exchange(sums, "z")
    combine = functools.partial(combine_kernel, heads, tokens, latent)
    return call(combine, (1, tokens, heads * 128), 3)(sums, values, other)


Y_SIZE = 4


def solution(mesh):
    batch, seq = mesh.shape["batch"], mesh.shape["seq"]
    mesh = Mesh(mesh.devices.reshape(batch, seq // Y_SIZE, Y_SIZE), ("batch", "z", "y"))
    both = ("z", "y")
    in_specs = (
        P("batch", None, both),
        P("batch", None, both),
        P("batch", both, None),
        P("batch"),
        P(both, "batch", None),
        P(both, "batch", None),
    )
    out_specs = P("batch", None, both)
    run = functools.partial(body, dict(mesh.shape))
    return jax.shard_map(run, mesh=mesh, in_specs=in_specs, out_specs=out_specs, check_vma=False)
```
